256 devices in a mesh: fsdp: 32 (over x, z), rep: 8 (over y, core).
Axes of the slice: x: 4, y: 4, z: 8, core: 2. Of those that a mesh axis runs over, the one named last changes fastest.
Arguments:
- grads: bfloat16 [8, 1024, 28672], P('rep', 'fsdp'), may hold values from -5 to 5
- owner: int32 [2, 56], replicated, may hold values from 0 to 31, as said below
- left_stats: float32 [8, 32, 2, 512, 512], P('rep', 'fsdp'), may hold values from -0.12 to 4, as said below
- right_stats: float32 [8, 32, 2, 512, 512], P('rep', 'fsdp'), may hold values from -0.12 to 4, as said below
- left_root: bfloat16 [8, 32, 2, 512, 512], P('rep', 'fsdp'), may hold values from -0.2 to 1.5, as said below
- right_root: bfloat16 [8, 32, 2, 512, 512], P('rep', 'fsdp'), may hold values from -0.2 to 1.5, as said below
Outputs:
- update: bfloat16 [1024, 28672], P('fsdp', 'rep')
- new_left: float32 [8, 32, 2, 512, 512], P('rep', 'fsdp')
- new_right: float32 [8, 32, 2, 512, 512], P('rep', 'fsdp')
The draws below stay inside these ranges and needn't reach their ends.
Inputs may be any that keep to these rules, and one draw needn't show every extreme that they name: In each block row the 7 block columns of one group (columns r * 7 to (r + 1) * 7 - 1) have distinct owners; in every group some owner holds a block in every block row. `left_stats`: each slot is symmetric. `right_stats`: each slot is symmetric. `left_root`: each slot is symmetric. `right_root`: each slot is symmetric.
All inputs are finite; a program needn't handle non-finite values.
Results may differ from the reference program's by a relative error of at most 0.022.
Values may be sent and summed in bfloat16 or wider, within the bound.
No kernel may reach another device: no remote copies, remote signals or barrier semaphores. Data moves between devices by JAX's collectives and lax.ppermute only.
A program may use at most 64 MiB of HBM per device.

```python
import jax
import jax.numpy as jnp
from jax import lax

BLOCK = 512
BR = 2
BC_REP = 7
BC = 56
ROWS = 1024
COLS = 28672
N_FSDP = 32
N_REP = 8


def draw_owner(key, part):
    key = jax.random.fold_in(key, 11)
    key_a, key_b, key_c = jax.random.split(key, 3)
    owner_scores = jax.random.randint(key_a, (BR, N_REP, N_FSDP), 0, 4096)
    preferred_owner = jax.random.randint(key_b, (N_REP,), 0, N_FSDP)
    extra_score = (jnp.arange(N_FSDP)[None, :] == preferred_owner[:, None]).astype(jnp.int32) * 8192
    owner_scores = (owner_scores + extra_score[None]) * N_FSDP + jnp.arange(N_FSDP, dtype=jnp.int32)
    picked = lax.top_k(owner_scores, BC_REP)[1].astype(jnp.int32)
    mixing_matrix = jax.random.randint(key_c, (BR, N_REP, BC_REP), 0, 4096) * BC_REP + jnp.arange(BC_REP, dtype=jnp.int32)
    order = jnp.argsort(mixing_matrix, axis=-1, stable=True)
    picked = jnp.take_along_axis(picked, order, axis=-1)
    return picked.reshape(BR, N_REP * BC_REP).astype(jnp.int32)


def symmetric_matrix(key, lo, hi, spread):
    key_a, key_b = jax.random.split(key)
    shape = (N_REP, N_FSDP, BR, BLOCK, BLOCK)
    raw = jnp.clip(jax.random.normal(key_a, shape, jnp.float32), -4.0, 4.0)
    diag = jnp.exp(jax.random.uniform(key_b, shape[:-1], jnp.float32, jnp.log(lo), jnp.log(hi)))
    off = (raw + jnp.swapaxes(raw, -1, -2)) * (0.7071 * spread)
    eye = jnp.eye(BLOCK, dtype=jnp.float32)
    return off * (1.0 - eye) + eye * diag[..., None, :]


def draw_left_stats(key, part):
    key = jax.random.fold_in(key, 21)
    return symmetric_matrix(key, 0.5, 4.0, 0.02)


def draw_right_stats(key, part):
    key = jax.random.fold_in(key, 22)
    return symmetric_matrix(key, 0.5, 4.0, 0.02)


def draw_left_root(key, part):
    key = jax.random.fold_in(key, 23)
    return symmetric_matrix(key, 0.5, 1.5, 0.03).astype(jnp.bfloat16)


def draw_right_root(key, part):
    key = jax.random.fold_in(key, 24)
    return symmetric_matrix(key, 0.5, 1.5, 0.03).astype(jnp.bfloat16)


def levels(own_key, shape, shards, least, top_value):
    loudness = 1.0
    for position, shards_of in shards:
        draws = jax.random.uniform(jax.random.fold_in(jax.random.fold_in(own_key, 6), position), (shards_of,), jnp.float32, least / len(shards), top_value / len(shards))
        loudness = loudness * jnp.repeat(jnp.exp(draws), shape[position] // shards_of).reshape((-1,) + (1,) * (len(shape) - 1 - position))
    return loudness


def scatter_about(rng, dims, width, reach, pieces=(), kind=jnp.bfloat16):
    values = width * jax.random.normal(rng, dims, jnp.float32)
    if pieces:
        values = values * levels(rng, dims, pieces, -0.22, 0.18)
    return jnp.clip(values, -reach, reach).astype(kind)


def setup_inputs(seed: int = 0) -> dict:
    key_list = jax.random.split(jax.random.key(seed), 7)
    grads = scatter_about(key_list[0], (N_REP, ROWS, COLS), 0.35, 5.0, ((0, 8), (1, 32)))
    owner = draw_owner(jax.random.fold_in(key_list[6], 71), 0)
    left_stats = draw_left_stats(jax.random.fold_in(key_list[6], 71), 0)
    right_stats = draw_right_stats(jax.random.fold_in(key_list[6], 71), 0)
    left_root = draw_left_root(jax.random.fold_in(key_list[6], 71), 0)
    right_root = draw_right_root(jax.random.fold_in(key_list[6], 71), 0)
    return {"grads": grads, "owner": owner, "left_stats": left_stats, "right_stats": right_stats, "left_root": left_root, "right_root": right_root}


BETA = 0.9
EPS = 1e-06

def one_block(items):
    g, left, right, lroot, rroot = items
    gram_left = jnp.dot(g, g.T, preferred_element_type=jnp.float32) / BLOCK
    gram_right = jnp.dot(g.T, g, preferred_element_type=jnp.float32) / BLOCK
    new_left = BETA * left + gram_left
    new_right = BETA * right + gram_right
    half = jnp.dot(lroot, g, preferred_element_type=jnp.float32).astype(jnp.bfloat16)
    pre = jnp.dot(half, rroot, preferred_element_type=jnp.float32)
    gfull = g.astype(jnp.float32)
    scale = jnp.sqrt(jnp.mean(gfull * gfull)) / jnp.sqrt(jnp.mean(pre * pre) + EPS)
    return ((scale * pre).astype(jnp.bfloat16), new_left, new_right)

def reference(grads, owner, left_stats, right_stats, left_root, right_root):
    total = lax.optimization_barrier(jnp.sum(grads.astype(jnp.float32), axis=0))
    grad_sum = total.astype(jnp.bfloat16)
    block_list = grad_sum.reshape(BR, BLOCK, BC, BLOCK).transpose(0, 2, 1, 3).reshape(BR * BC, BLOCK, BLOCK)
    index_of_row = jnp.repeat(jnp.arange(BR, dtype=jnp.int32), BC)
    col_index = jnp.tile(jnp.arange(BC, dtype=jnp.int32), BR)
    group_index = col_index // BC_REP
    owner_index = owner.reshape(-1).astype(jnp.int32)
    lefts = left_stats[group_index, owner_index, index_of_row]
    rights = right_stats[group_index, owner_index, index_of_row]
    lroots = left_root[group_index, owner_index, index_of_row]
    rroots = right_root[group_index, owner_index, index_of_row]
    outs, new_l, new_r = lax.map(one_block, (block_list, lefts, rights, lroots, rroots))
    new_left = (BETA * left_stats).at[group_index, owner_index, index_of_row].set(new_l)
    new_right = (BETA * right_stats).at[group_index, owner_index, index_of_row].set(new_r)
    update = outs.reshape(BR, BC, BLOCK, BLOCK).transpose(0, 2, 1, 3).reshape(ROWS, COLS)
    return (update, new_left, new_right)
```

```python
import jax
import jax.numpy as jnp
from jax import lax
from jax.sharding import PartitionSpec as P

BETA = 0.9
EPS = 1e-06


def precondition(g, left, right, lroot, rroot):
    block = g.shape[0]
    gram_left = (
        lax.dot_general(g, g, (((1,), (1,)), ((), ())), preferred_element_type=jnp.float32) / block
    )
    gram_right = (
        lax.dot_general(g, g, (((0,), (0,)), ((), ())), preferred_element_type=jnp.float32) / block
    )
    new_left = BETA * left + gram_left
    new_right = BETA * right + gram_right
    half = jnp.dot(lroot, g, preferred_element_type=jnp.float32).astype(jnp.bfloat16)
    pre = jnp.dot(half, rroot, preferred_element_type=jnp.float32)
    gfull = g.astype(jnp.float32)
    scale = jnp.sqrt(jnp.mean(gfull * gfull)) / jnp.sqrt(jnp.mean(pre * pre) + EPS)
    return ((scale * pre).astype(jnp.bfloat16), new_left, new_right)


def sum_over_rep(shard, width):
    n_rep = lax.axis_size("rep")
    rep_index = lax.axis_index("rep")
    core = rep_index % 2
    ring = n_rep // 2
    y_index = rep_index // 2

    def group(array, index):
        return lax.dynamic_slice_in_dim(array, index * width, width, 1)

    sent = jnp.concatenate([group(shard, 2 * i + 1 - core) for i in range(ring)], axis=1)
    other = lax.ppermute(sent, "rep", [(i, i + 1 - 2 * (i % 2)) for i in range(n_rep)])
    parts = []
    for step in range(ring):
        target = (y_index + step) % ring
        mine = group(shard, 2 * target + core).astype(jnp.float32)
        parts.append(mine + group(other, target).astype(jnp.float32))
    total = parts[0]
    arrived = [
        lax.ppermute(
            parts[step].astype(jnp.bfloat16),
            "rep",
            [(i, (i + 2 * step) % n_rep) for i in range(n_rep)],
        )
        for step in range(1, ring)
    ]
    for part in arrived:
        total = total + part.astype(jnp.float32)
    return total.astype(jnp.bfloat16)


def on_device(grads, owner, left_stats, right_stats, left_root, right_root):
    strip = grads.shape[1]
    n_fsdp = lax.axis_size("fsdp")
    n_rep = lax.axis_size("rep")
    block = left_stats.shape[-1]
    slots = left_stats.shape[2]
    width = grads.shape[2] // n_rep
    group_list = width // block
    rep_index = lax.axis_index("rep")
    fsdp_index = lax.axis_index("fsdp")
    grad_part = sum_over_rep(grads[0], width)
    block_row = fsdp_index * strip // block
    owner_row = lax.dynamic_index_in_dim(owner, block_row, 0, keepdims=False)
    owner_cols = lax.dynamic_slice_in_dim(owner_row, rep_index * group_list, group_list, 0)
    select = (jnp.arange(n_fsdp, dtype=jnp.int32)[:, None] == owner_cols[None, :]).astype(
        jnp.bfloat16
    )
    pieces = grad_part.reshape(strip, group_list, block)
    outgoing = jnp.einsum("oc,scd->osd", select, pieces, preferred_element_type=jnp.float32).astype(
        jnp.bfloat16
    )
    incoming = lax.all_to_all(outgoing, "fsdp", split_axis=0, concat_axis=0, tiled=True)
    block_list = incoming.reshape(slots, block, block)
    lefts = left_stats[0, 0]
    rights = right_stats[0, 0]
    lroots = left_root[0, 0]
    rroots = right_root[0, 0]
    results, new_l, new_r = jax.vmap(precondition)(block_list, lefts, rights, lroots, rroots)
    going_back = results.reshape(n_fsdp, strip, block)
    returned = lax.all_to_all(going_back, "fsdp", split_axis=0, concat_axis=0, tiled=True)
    placed = jnp.einsum("oc,osd->scd", select, returned, preferred_element_type=jnp.float32).astype(
        jnp.bfloat16
    )
    update = placed.reshape(strip, width)
    return (update, new_l[None, None], new_r[None, None])


def solution(mesh):
    in_specs = (
        P("rep", "fsdp", None),
        P(),
        P("rep", "fsdp", None, None, None),
        P("rep", "fsdp", None, None, None),
        P("rep", "fsdp", None, None, None),
        P("rep", "fsdp", None, None, None),
    )
    out_specs = (
        P("fsdp", "rep"),
        P("rep", "fsdp", None, None, None),
        P("rep", "fsdp", None, None, None),
    )
    return jax.shard_map(
        on_device, mesh=mesh, in_specs=in_specs, out_specs=out_specs, check_vma=False
    )
```

```python
import functools

import jax
import jax.numpy as jnp
from jax import lax
from jax.experimental import pallas as pl
from jax.experimental.pallas import tpu as pltpu
from jax.sharding import PartitionSpec as P

BETA = 0.9
EPS = 1e-06
VMEM_LIMIT = 24 * 1024 * 1024
ANY = pl.BlockSpec(memory_space=pl.ANY)
VMEM = pl.BlockSpec(memory_space=pltpu.VMEM)
SMEM = pl.BlockSpec(memory_space=pltpu.SMEM)


def params(**kw):
    return pltpu.CompilerParams(vmem_limit_bytes=VMEM_LIMIT, **kw)


def pack_kernel(ring, width, place, shard, sent, sems):
    core = place[1]
    copies = []
    for i in range(ring):
        start = pl.multiple_of((2 * i + 1 - core) * width, width)
        copies.append(
            pltpu.make_async_copy(shard.at[:, pl.ds(start, width)], sent.at[i], sems.at[i])
        )
    for copy in copies:
        copy.start()
    for copy in copies:
        copy.wait()


def pack(shard, place, ring, width):
    return pl.pallas_call(
        functools.partial(pack_kernel, ring, width),
        out_shape=jax.ShapeDtypeStruct((ring, shard.shape[0], width), shard.dtype),
        in_specs=[SMEM, ANY],
        out_specs=ANY,
        scratch_shapes=[pltpu.SemaphoreType.DMA((ring,))],
        compiler_params=params(),
        name="pack",
    )(place, shard)


def pair_kernel(ring, width, place, shard, other, *rest):
    outs, (mine, theirs, sems) = rest[:ring], rest[ring:]
    y_index, core = place[0], place[1]
    copies = []
    for step in range(ring):
        target = lax.rem(y_index + step, ring)
        start = pl.multiple_of((2 * target + core) * width, width)
        copies.append(
            (
                pltpu.make_async_copy(
                    shard.at[:, pl.ds(start, width)], mine.at[step], sems.at[0, step]
                ),
                pltpu.make_async_copy(other.at[target], theirs.at[step], sems.at[1, step]),
            )
        )
    order = list(range(1, ring)) + [0]
    for step in order:
        for copy in copies[step]:
            copy.start()
    for step in order:
        for copy in copies[step]:
            copy.wait()
        total = mine[step].astype(jnp.float32) + theirs[step].astype(jnp.float32)
        outs[step][...] = total.astype(outs[step].dtype)


def pair_sum(shard, other, place, ring, width):
    strip = shard.shape[0]
    shapes = [
        jax.ShapeDtypeStruct((strip, width), jnp.bfloat16 if step else jnp.float32)
        for step in range(ring)
    ]
    return pl.pallas_call(
        functools.partial(pair_kernel, ring, width),
        out_shape=shapes,
        in_specs=[SMEM, ANY, ANY],
        out_specs=[VMEM] * ring,
        scratch_shapes=[
            pltpu.VMEM((ring, strip, width), jnp.bfloat16),
            pltpu.VMEM((ring, strip, width), jnp.bfloat16),
            pltpu.SemaphoreType.DMA((2, ring)),
        ],
        compiler_params=params(),
        name="pair_sum",
    )(place, shard, other)


def slots_kernel(pieces, block, owners, *refs):
    out = refs[-1]
    out[...] = jnp.zeros_like(out)
    for c in range(pieces):
        columns = slice(c * block, (c + 1) * block)
        total = refs[0][:, columns]
        for part in refs[1:-1]:
            total = total + part[:, columns].astype(jnp.float32)
        out[owners[c]] = total.astype(jnp.bfloat16)


def fill_slots(parts, owners, n_fsdp, block):
    strip, width = parts[0].shape
    return pl.pallas_call(
        functools.partial(slots_kernel, width // block, block),
        out_shape=jax.ShapeDtypeStruct((n_fsdp, strip, block), jnp.bfloat16),
        in_specs=[SMEM] + [VMEM] * len(parts),
        out_specs=VMEM,
        compiler_params=params(),
        name="fill_slots",
    )(owners, *parts)


def precondition_kernel(block, g_ref, l_ref, r_ref, out_ref):
    g = g_ref[...].reshape(block, block)
    half = jnp.dot(l_ref[0], g, preferred_element_type=jnp.float32).astype(jnp.bfloat16)
    pre = jnp.dot(half, r_ref[0], preferred_element_type=jnp.float32)
    gfull = g.astype(jnp.float32)
    scale = jnp.sqrt(jnp.mean(gfull * gfull)) / jnp.sqrt(jnp.mean(pre * pre) + EPS)
    out_ref[...] = (scale * pre).astype(jnp.bfloat16).reshape(out_ref.shape)


def precondition(incoming, lroots, rroots):
    n, strip, block = incoming.shape
    slots = lroots.shape[0]
    rows = pl.BlockSpec((n // slots, strip, block), lambda s: (s, 0, 0))
    root = pl.BlockSpec((1, block, block), lambda s: (s, 0, 0))
    return pl.pallas_call(
        functools.partial(precondition_kernel, block),
        out_shape=jax.ShapeDtypeStruct(incoming.shape, jnp.bfloat16),
        grid=(slots,),
        in_specs=[rows, root, root],
        out_specs=rows,
        compiler_params=params(),
        cost_estimate=pl.CostEstimate(
            flops=4 * slots * block**3, bytes_accessed=8 * slots * block**2, transcendentals=0
        ),
        name="precondition",
    )(incoming, lroots, rroots)


def collect_kernel(pieces, block, owners, returned, update, sems):
    copies = [
        pltpu.make_async_copy(
            returned.at[owners[c]], update.at[:, pl.ds(c * block, block)], sems.at[c]
        )
        for c in range(pieces)
    ]
    for copy in copies:
        copy.start()
    for copy in copies:
        copy.wait()


def collect(returned, owners, pieces):
    n, strip, block = returned.shape
    return pl.pallas_call(
        functools.partial(collect_kernel, pieces, block),
        out_shape=jax.ShapeDtypeStruct((strip, pieces * block), returned.dtype),
        in_specs=[SMEM, ANY],
        out_specs=ANY,
        scratch_shapes=[pltpu.SemaphoreType.DMA((pieces,))],
        compiler_params=params(),
        name="collect",
    )(owners, returned)


def statistics(g, left, right):
    block = g.shape[0]
    gram_left = (
        lax.dot_general(g, g, (((1,), (1,)), ((), ())), preferred_element_type=jnp.float32) / block
    )
    gram_right = (
        lax.dot_general(g, g, (((0,), (0,)), ((), ())), preferred_element_type=jnp.float32) / block
    )
    return BETA * left + gram_left, BETA * right + gram_right


def on_device(grads, owner, left_stats, right_stats, left_root, right_root):
    strip = grads.shape[1]
    n_fsdp = lax.axis_size("fsdp")
    n_rep = lax.axis_size("rep")
    block = left_stats.shape[-1]
    slots = left_stats.shape[2]
    width = grads.shape[2] // n_rep
    pieces = width // block
    ring = n_rep // 2
    rep_index = lax.axis_index("rep")
    fsdp_index = lax.axis_index("fsdp")
    place = jnp.stack([rep_index // 2, rep_index % 2]).astype(jnp.int32)
    owners = lax.dynamic_slice(
        owner, (fsdp_index * strip // block, rep_index * pieces), (1, pieces)
    )[0]

    shard = grads[0]
    sent = pack(shard, place, ring, width)
    other = lax.ppermute(sent, "rep", [(i, i + 1 - 2 * (i % 2)) for i in range(n_rep)])
    parts = pair_sum(shard, other, place, ring, width)
    arrived = [
        lax.ppermute(parts[step], "rep", [(i, (i + 2 * step) % n_rep) for i in range(n_rep)])
        for step in range(1, ring)
    ]
    outgoing = fill_slots([parts[0], *arrived], owners, n_fsdp, block)
    incoming = lax.all_to_all(outgoing, "fsdp", split_axis=0, concat_axis=0, tiled=True)
    results = precondition(incoming, left_root[0, 0], right_root[0, 0])
    returned = lax.all_to_all(results, "fsdp", split_axis=0, concat_axis=0, tiled=True)
    new_l, new_r = jax.vmap(statistics)(
        incoming.reshape(slots, block, block), left_stats[0, 0], right_stats[0, 0]
    )
    update = collect(returned, owners, pieces)
    return (update, new_l[None, None], new_r[None, None])


def solution(mesh):
    in_specs = (
        P("rep", "fsdp", None),
        P(),
        P("rep", "fsdp", None, None, None),
        P("rep", "fsdp", None, None, None),
        P("rep", "fsdp", None, None, None),
        P("rep", "fsdp", None, None, None),
    )
    out_specs = (
        P("fsdp", "rep"),
        P("rep", "fsdp", None, None, None),
        P("rep", "fsdp", None, None, None),
    )
    return jax.shard_map(
        on_device, mesh=mesh, in_specs=in_specs, out_specs=out_specs, check_vma=False
    )
```

```python
import functools

import jax
import jax.numpy as jnp
from jax import lax
from jax.experimental import pallas as pl
from jax.experimental.pallas import tpu as pltpu
from jax.sharding import PartitionSpec as P

BETA = 0.9
EPS = 1e-06
TOKEN = (16, 128)
Y_ORDER = (2, 1, 3)
VMEM_LIMIT = 24 * 1024 * 1024
ANY = pl.BlockSpec(memory_space=pl.ANY)
HBM = pl.BlockSpec(memory_space=pltpu.HBM)
VMEM = pl.BlockSpec(memory_space=pltpu.VMEM)
CHEAP = pl.CostEstimate(flops=1, bytes_accessed=1, transcendentals=0)
COPY = pl.CostEstimate(flops=1, bytes_accessed=2**21, transcendentals=0)
SMEM = pl.BlockSpec(memory_space=pltpu.SMEM)


def params(**kw):
    return pltpu.CompilerParams(vmem_limit_bytes=VMEM_LIMIT, **kw)


def groups_kernel(ring, width, other, shard, *refs):
    out, sems = refs[-2:]
    rep_index = lax.axis_index("rep")
    core = lax.rem(rep_index, 2)
    if other:
        core = 1 - core
    copies = []
    for step in range(ring):
        target = lax.rem(rep_index // 2 + step, ring)
        start = pl.multiple_of((2 * target + core) * width, width)
        copies.append(
            pltpu.make_async_copy(shard.at[:, pl.ds(start, width)], out.at[step], sems.at[step])
        )
    for copy in copies:
        copy.start()
    for copy in copies:
        copy.wait()


def groups(shard, ring, width, other, *after):
    return pl.pallas_call(
        functools.partial(groups_kernel, ring, width, other),
        out_shape=jax.ShapeDtypeStruct((ring, shard.shape[0], width), shard.dtype),
        in_specs=[HBM] + [ANY] * len(after),
        out_specs=VMEM,
        scratch_shapes=[pltpu.SemaphoreType.DMA((ring,))],
        compiler_params=params(),
        cost_estimate=COPY,
        name="groups",
    )(pltpu.with_memory_space_constraint(shard, pltpu.HBM), *after)


def pair_kernel(ring, kept, other, *refs):
    outs = refs[-ring:]
    for step in range(ring):
        outs[step][...] = kept[step] + other[step]


def pair_sum(kept, other, *after):
    ring = kept.shape[0]
    return pl.pallas_call(
        functools.partial(pair_kernel, ring),
        out_shape=[jax.ShapeDtypeStruct(kept.shape[1:], kept.dtype)] * ring,
        in_specs=[VMEM, VMEM] + [ANY] * len(after),
        out_specs=[VMEM] * ring,
        compiler_params=params(),
        cost_estimate=CHEAP,
        name="pair_sum",
    )(kept, other, *after)


def total_of(parts, columns):
    total = parts[0][:, columns].astype(jnp.float32)
    for part in parts[1:]:
        total = total + part[:, columns].astype(jnp.float32)
    return total.astype(jnp.bfloat16)


def total_kernel(block, *refs):
    out, token = refs[-2:]
    for c in range(out.shape[1] // block):
        columns = slice(c * block, (c + 1) * block)
        out[:, columns] = total_of(refs[:-2], columns)
    token[...] = jnp.zeros_like(token)


def add_up(parts, block):
    return pl.pallas_call(
        functools.partial(total_kernel, block),
        out_shape=[
            jax.ShapeDtypeStruct(parts[0].shape, jnp.bfloat16),
            jax.ShapeDtypeStruct(TOKEN, jnp.bfloat16),
        ],
        in_specs=[VMEM] * len(parts),
        out_specs=[VMEM] * 2,
        compiler_params=params(),
        cost_estimate=CHEAP,
        name="add_up",
    )(*parts)


def slots_kernel(pieces, block, n_parts, owners, *refs):
    parts, out = refs[:n_parts], refs[-1]
    out[...] = jnp.zeros_like(out)
    for c in range(pieces):
        out[owners[c]] = total_of(parts, slice(c * block, (c + 1) * block))


def fill_slots(parts, owners, n_fsdp, block, *after):
    strip, width = parts[0].shape
    return pl.pallas_call(
        functools.partial(slots_kernel, width // block, block, len(parts)),
        out_shape=jax.ShapeDtypeStruct((n_fsdp, strip, block), jnp.bfloat16),
        in_specs=[SMEM] + [VMEM] * len(parts) + [ANY] * len(after),
        out_specs=VMEM,
        compiler_params=params(),
        cost_estimate=CHEAP,
        name="fill_slots",
    )(owners, *parts, *after)


def precondition_kernel(g_ref, l_ref, r_ref, out_ref):
    slots, block, _ = l_ref.shape
    rows = g_ref.shape[0] // slots
    for b in range(slots):
        g = g_ref[b * rows : (b + 1) * rows].reshape(block, block)
        half = jnp.dot(l_ref[b], g, preferred_element_type=jnp.float32).astype(jnp.bfloat16)
        pre = jnp.dot(half, r_ref[b], preferred_element_type=jnp.float32)
        gfull = g.astype(jnp.float32)
        scale = jnp.sqrt(jnp.mean(gfull * gfull)) / jnp.sqrt(jnp.mean(pre * pre) + EPS)
        out_ref[b * rows : (b + 1) * rows] = (
            (scale * pre).astype(jnp.bfloat16).reshape(rows, *g_ref.shape[1:])
        )


def precondition(incoming, lroots, rroots):
    slots, block, _ = lroots.shape
    return pl.pallas_call(
        precondition_kernel,
        out_shape=jax.ShapeDtypeStruct(incoming.shape, jnp.bfloat16),
        in_specs=[VMEM] * 3,
        out_specs=VMEM,
        compiler_params=params(),
        cost_estimate=pl.CostEstimate(
            flops=4 * slots * block**3, bytes_accessed=8 * slots * block**2, transcendentals=0
        ),
        name="precondition",
    )(incoming, lroots, rroots)


def collect_kernel(pieces, block, owners, returned, update, sems):
    copies = [
        pltpu.make_async_copy(
            returned.at[owners[c]], update.at[:, pl.ds(c * block, block)], sems.at[c]
        )
        for c in range(pieces)
    ]
    for copy in copies:
        copy.start()
    for copy in copies:
        copy.wait()


def collect(returned, owners, pieces):
    n, strip, block = returned.shape
    return pl.pallas_call(
        functools.partial(collect_kernel, pieces, block),
        out_shape=jax.ShapeDtypeStruct((strip, pieces * block), returned.dtype),
        in_specs=[SMEM, ANY],
        out_specs=ANY,
        scratch_shapes=[pltpu.SemaphoreType.DMA((pieces,))],
        compiler_params=params(),
        name="collect",
    )(owners, returned)


def statistics(g, left, right):
    block = g.shape[0]
    gram_left = (
        lax.dot_general(g, g, (((1,), (1,)), ((), ())), preferred_element_type=jnp.float32) / block
    )
    gram_right = (
        lax.dot_general(g, g, (((0,), (0,)), ((), ())), preferred_element_type=jnp.float32) / block
    )
    return BETA * left + gram_left, BETA * right + gram_right


def on_device(grads, owner, left_stats, right_stats, left_root, right_root):
    strip = grads.shape[1]
    n_fsdp = lax.axis_size("fsdp")
    n_rep = lax.axis_size("rep")
    block = left_stats.shape[-1]
    slots = left_stats.shape[2]
    width = grads.shape[2] // n_rep
    pieces = width // block
    ring = n_rep // 2
    rep_index = lax.axis_index("rep")
    fsdp_index = lax.axis_index("fsdp")
    owners = lax.dynamic_slice(
        owner, (fsdp_index * strip // block, rep_index * pieces), (1, pieces)
    )[0]

    core = rep_index % 2
    swap = [(i, i + 1 - 2 * (i % 2)) for i in range(n_rep)]
    other = lax.ppermute(groups(grads[0], ring, width, True), "rep", swap)
    parts = pair_sum(groups(grads[0], ring, width, False), other)

    def along_y(parts):
        arrived = [
            lax.ppermute(parts[step], "rep", [(i, (i + 2 * step) % n_rep) for i in range(n_rep)])
            for step in Y_ORDER
        ]
        return [parts[0], *arrived]

    total, token = lax.cond(
        core == 0,
        lambda parts: tuple(add_up(along_y(parts), block)),
        lambda parts: (parts[0], jnp.zeros(TOKEN, jnp.bfloat16)),
        parts,
    )
    token = lax.ppermute(token, "rep", swap)
    outgoing = lax.cond(
        core == 1,
        lambda parts, total, token, owners: fill_slots(
            along_y(parts), owners, n_fsdp, block, token
        ),
        lambda parts, total, token, owners: fill_slots([total], owners, n_fsdp, block),
        parts, total, token, owners,
    )
    incoming = lax.all_to_all(outgoing, "fsdp", split_axis=0, concat_axis=0, tiled=True)
    results = precondition(incoming, left_root[0, 0], right_root[0, 0])
    returned = lax.all_to_all(results, "fsdp", split_axis=0, concat_axis=0, tiled=True)
    new_l, new_r = jax.vmap(statistics)(
        incoming.reshape(slots, block, block), left_stats[0, 0], right_stats[0, 0]
    )
    update = collect(returned, owners, pieces)
    return (update, new_l[None, None], new_r[None, None])


def solution(mesh):
    in_specs = (
        P("rep", "fsdp", None),
        P(),
        P("rep", "fsdp", None, None, None),
        P("rep", "fsdp", None, None, None),
        P("rep", "fsdp", None, None, None),
        P("rep", "fsdp", None, None, None),
    )
    out_specs = (
        P("fsdp", "rep"),
        P("rep", "fsdp", None, None, None),
        P("rep", "fsdp", None, None, None),
    )
    return jax.shard_map(
        on_device, mesh=mesh, in_specs=in_specs, out_specs=out_specs, check_vma=False
    )
```

```python
import functools

import jax
import jax.numpy as jnp
from jax import lax
from jax.experimental import pallas as pl
from jax.experimental.pallas import tpu as pltpu
from jax.sharding import PartitionSpec as P

BETA = 0.9
EPS = 1e-06
RING_ROWS = 16
Y_ORDER = (2, 1, 3)
VMEM_LIMIT = 24 * 1024 * 1024
ANY = pl.BlockSpec(memory_space=pl.ANY)
HBM = pl.BlockSpec(memory_space=pltpu.HBM)
VMEM = pl.BlockSpec(memory_space=pltpu.VMEM)
CHEAP = pl.CostEstimate(flops=1, bytes_accessed=1, transcendentals=0)
COPY = pl.CostEstimate(flops=1, bytes_accessed=2**21, transcendentals=0)
SMEM = pl.BlockSpec(memory_space=pltpu.SMEM)


def params(**kw):
    return pltpu.CompilerParams(vmem_limit_bytes=VMEM_LIMIT, **kw)


def groups_kernel(ring, width, other, shard, *refs):
    out, sems = refs[-2:]
    rep_index = lax.axis_index("rep")
    core = lax.rem(rep_index, 2)
    if other:
        core = 1 - core
    copies = []
    for step in range(ring):
        target = lax.rem(rep_index // 2 + step, ring)
        start = pl.multiple_of((2 * target + core) * width, width)
        copies.append(
            pltpu.make_async_copy(shard.at[:, pl.ds(start, width)], out.at[step], sems.at[step])
        )
    for copy in copies:
        copy.start()
    for copy in copies:
        copy.wait()


def groups(shard, ring, width, other, *after):
    return pl.pallas_call(
        functools.partial(groups_kernel, ring, width, other),
        out_shape=jax.ShapeDtypeStruct((ring, shard.shape[0], width), shard.dtype),
        in_specs=[HBM] + [ANY] * len(after),
        out_specs=VMEM,
        scratch_shapes=[pltpu.SemaphoreType.DMA((ring,))],
        compiler_params=params(),
        cost_estimate=COPY,
        name="groups",
    )(pltpu.with_memory_space_constraint(shard, pltpu.HBM), *after)


def pair_kernel(ring, kept, other, *refs):
    outs = refs[-ring:]
    for step in range(ring):
        outs[step][...] = kept[step] + other[step]


def pair_sum(kept, other, *after):
    ring = kept.shape[0]
    return pl.pallas_call(
        functools.partial(pair_kernel, ring),
        out_shape=[jax.ShapeDtypeStruct(kept.shape[1:], kept.dtype)] * ring,
        in_specs=[VMEM, VMEM] + [ANY] * len(after),
        out_specs=[VMEM] * ring,
        compiler_params=params(),
        cost_estimate=CHEAP,
        name="pair_sum",
    )(kept, other, *after)


def total_of(parts, columns):
    total = parts[0][:, columns].astype(jnp.float32)
    for part in parts[1:]:
        total = total + part[:, columns].astype(jnp.float32)
    return total.astype(jnp.bfloat16)


def total_kernel(block, *refs):
    out = refs[-1]
    for c in range(out.shape[1] // block):
        columns = slice(c * block, (c + 1) * block)
        out[:, columns] = total_of(refs[:-1], columns)


def add_up(parts, block):
    return pl.pallas_call(
        functools.partial(total_kernel, block),
        out_shape=jax.ShapeDtypeStruct(parts[0].shape, jnp.bfloat16),
        in_specs=[VMEM] * len(parts),
        out_specs=VMEM,
        compiler_params=params(),
        cost_estimate=CHEAP,
        name="add_up",
    )(*parts)


def rows_kernel(start, rows, part, *refs):
    out = refs[-1]
    out[...] = part[start : start + rows]


def take_rows(part, start, rows, *after):
    return pl.pallas_call(
        functools.partial(rows_kernel, start, rows),
        out_shape=jax.ShapeDtypeStruct((rows, part.shape[1]), part.dtype),
        in_specs=[VMEM] + [ANY] * len(after),
        out_specs=VMEM,
        compiler_params=params(),
        cost_estimate=CHEAP,
        name="take_rows",
    )(part, *after)


def plus_kernel(start, part, running, out):
    out[...] = part[start : start + running.shape[0]] + running[...]


def plus(part, start, running):
    return pl.pallas_call(
        functools.partial(plus_kernel, start),
        out_shape=jax.ShapeDtypeStruct(running.shape, running.dtype),
        in_specs=[VMEM] * 2,
        out_specs=VMEM,
        compiler_params=params(),
        cost_estimate=CHEAP,
        name="plus",
    )(part, running)


def join_kernel(*refs):
    start = 0
    for ref in refs[:-1]:
        refs[-1][start : start + ref.shape[0]] = ref[...]
        start += ref.shape[0]


def join(pieces):
    rows = sum(piece.shape[0] for piece in pieces)
    return pl.pallas_call(
        join_kernel,
        out_shape=jax.ShapeDtypeStruct((rows, pieces[0].shape[1]), pieces[0].dtype),
        in_specs=[VMEM] * len(pieces),
        out_specs=VMEM,
        compiler_params=params(),
        cost_estimate=CHEAP,
        name="join",
    )(*pieces)


def slots_kernel(pieces, block, n_parts, owners, *refs):
    parts, out = refs[:n_parts], refs[-1]
    out[...] = jnp.zeros_like(out)
    for c in range(pieces):
        out[owners[c]] = total_of(parts, slice(c * block, (c + 1) * block))


def fill_slots(parts, owners, n_fsdp, block, *after):
    strip, width = parts[0].shape
    return pl.pallas_call(
        functools.partial(slots_kernel, width // block, block, len(parts)),
        out_shape=jax.ShapeDtypeStruct((n_fsdp, strip, block), jnp.bfloat16),
        in_specs=[SMEM] + [VMEM] * len(parts) + [ANY] * len(after),
        out_specs=VMEM,
        compiler_params=params(),
        cost_estimate=CHEAP,
        name="fill_slots",
    )(owners, *parts, *after)


def precondition_kernel(g_ref, l_ref, r_ref, out_ref):
    slots, block, _ = l_ref.shape
    rows = g_ref.shape[0] // slots
    for b in range(slots):
        g = g_ref[b * rows : (b + 1) * rows].reshape(block, block)
        half = jnp.dot(l_ref[b], g, preferred_element_type=jnp.float32).astype(jnp.bfloat16)
        pre = jnp.dot(half, r_ref[b], preferred_element_type=jnp.float32)
        gfull = g.astype(jnp.float32)
        scale = jnp.sqrt(jnp.mean(gfull * gfull)) / jnp.sqrt(jnp.mean(pre * pre) + EPS)
        out_ref[b * rows : (b + 1) * rows] = (
            (scale * pre).astype(jnp.bfloat16).reshape(rows, *g_ref.shape[1:])
        )


def precondition(incoming, lroots, rroots):
    slots, block, _ = lroots.shape
    return pl.pallas_call(
        precondition_kernel,
        out_shape=jax.ShapeDtypeStruct(incoming.shape, jnp.bfloat16),
        in_specs=[VMEM] * 3,
        out_specs=VMEM,
        compiler_params=params(),
        cost_estimate=pl.CostEstimate(
            flops=4 * slots * block**3, bytes_accessed=8 * slots * block**2, transcendentals=0
        ),
        name="precondition",
    )(incoming, lroots, rroots)


def collect_kernel(pieces, block, owners, returned, update, sems):
    copies = [
        pltpu.make_async_copy(
            returned.at[owners[c]], update.at[:, pl.ds(c * block, block)], sems.at[c]
        )
        for c in range(pieces)
    ]
    for copy in copies:
        copy.start()
    for copy in copies:
        copy.wait()


def collect(returned, owners, pieces):
    n, strip, block = returned.shape
    return pl.pallas_call(
        functools.partial(collect_kernel, pieces, block),
        out_shape=jax.ShapeDtypeStruct((strip, pieces * block), returned.dtype),
        in_specs=[SMEM, ANY],
        out_specs=ANY,
        scratch_shapes=[pltpu.SemaphoreType.DMA((pieces,))],
        compiler_params=params(),
        name="collect",
    )(owners, returned)


def statistics(g, left, right):
    block = g.shape[0]
    gram_left = (
        lax.dot_general(g, g, (((1,), (1,)), ((), ())), preferred_element_type=jnp.float32) / block
    )
    gram_right = (
        lax.dot_general(g, g, (((0,), (0,)), ((), ())), preferred_element_type=jnp.float32) / block
    )
    return BETA * left + gram_left, BETA * right + gram_right


def on_device(grads, owner, left_stats, right_stats, left_root, right_root):
    strip = grads.shape[1]
    n_fsdp = lax.axis_size("fsdp")
    n_rep = lax.axis_size("rep")
    block = left_stats.shape[-1]
    slots = left_stats.shape[2]
    width = grads.shape[2] // n_rep
    pieces = width // block
    ring = n_rep // 2
    rep_index = lax.axis_index("rep")
    fsdp_index = lax.axis_index("fsdp")
    owners = lax.dynamic_slice(
        owner, (fsdp_index * strip // block, rep_index * pieces), (1, pieces)
    )[0]

    swap = [(i, i + 1 - 2 * (i % 2)) for i in range(n_rep)]
    other = lax.ppermute(groups(grads[0], ring, width, True), "rep", swap)
    parts = pair_sum(groups(grads[0], ring, width, False), other)

    def send_y(array, step):
        return lax.ppermute(array, "rep", [(i, (i + 2 * step) % n_rep) for i in range(n_rep)])

    def directly(parts):
        return add_up([parts[0]] + [send_y(parts[step], step) for step in Y_ORDER], block)

    def round_ring(parts):
        running = take_rows(parts[-1], 0, RING_ROWS)
        for part in parts[-2::-1]:
            running = plus(part, 0, send_y(running, 1))
        rest = [take_rows(part, RING_ROWS, strip - RING_ROWS, running) for part in parts]
        rest = add_up([rest[0]] + [send_y(rest[step], step) for step in Y_ORDER], block)
        return join([running, rest])

    total = lax.cond(rep_index % 2 == 0, directly, round_ring, parts)
    outgoing = fill_slots([total], owners, n_fsdp, block)
    incoming = lax.all_to_all(outgoing, "fsdp", split_axis=0, concat_axis=0, tiled=True)
    results = precondition(incoming, left_root[0, 0], right_root[0, 0])
    returned = lax.all_to_all(results, "fsdp", split_axis=0, concat_axis=0, tiled=True)
    new_l, new_r = jax.vmap(statistics)(
        incoming.reshape(slots, block, block), left_stats[0, 0], right_stats[0, 0]
    )
    update = collect(returned, owners, pieces)
    return (update, new_l[None, None], new_r[None, None])


def solution(mesh):
    in_specs = (
        P("rep", "fsdp", None),
        P(),
        P("rep", "fsdp", None, None, None),
        P("rep", "fsdp", None, None, None),
        P("rep", "fsdp", None, None, None),
        P("rep", "fsdp", None, None, None),
    )
    out_specs = (
        P("fsdp", "rep"),
        P("rep", "fsdp", None, None, None),
        P("rep", "fsdp", None, None, None),
    )
    return jax.shard_map(
        on_device, mesh=mesh, in_specs=in_specs, out_specs=out_specs, check_vma=False
    )
```

```python
import functools

import jax
import jax.numpy as jnp
from jax import lax
from jax.experimental import pallas as pl
from jax.experimental.pallas import tpu as pltpu
from jax.sharding import PartitionSpec as P

BETA = 0.9
EPS = 1e-06
Y_ORDER = (2, 1, 3)
VMEM_LIMIT = 24 * 1024 * 1024
ANY = pl.BlockSpec(memory_space=pl.ANY)
HBM = pl.BlockSpec(memory_space=pltpu.HBM)
VMEM = pl.BlockSpec(memory_space=pltpu.VMEM)
CHEAP = pl.CostEstimate(flops=1, bytes_accessed=1, transcendentals=0)
COPY = pl.CostEstimate(flops=1, bytes_accessed=2**21, transcendentals=0)
SMEM = pl.BlockSpec(memory_space=pltpu.SMEM)


def params(**kw):
    return pltpu.CompilerParams(vmem_limit_bytes=VMEM_LIMIT, **kw)


def groups_kernel(ring, width, other, shard, *refs):
    out, sems = refs[-2:]
    rep_index = lax.axis_index("rep")
    core = lax.rem(rep_index, 2)
    if other:
        core = 1 - core
    copies = []
    for step in range(ring):
        target = lax.rem(rep_index // 2 + step, ring)
        start = pl.multiple_of((2 * target + core) * width, width)
        copies.append(
            pltpu.make_async_copy(shard.at[:, pl.ds(start, width)], out.at[step], sems.at[step])
        )
    for copy in copies:
        copy.start()
    for copy in copies:
        copy.wait()


def groups(shard, ring, width, other, *after):
    return pl.pallas_call(
        functools.partial(groups_kernel, ring, width, other),
        out_shape=jax.ShapeDtypeStruct((ring, shard.shape[0], width), shard.dtype),
        in_specs=[HBM] + [ANY] * len(after),
        out_specs=VMEM,
        scratch_shapes=[pltpu.SemaphoreType.DMA((ring,))],
        compiler_params=params(),
        cost_estimate=COPY,
        name="groups",
    )(pltpu.with_memory_space_constraint(shard, pltpu.HBM), *after)


def pair_kernel(ring, kept, other, *refs):
    outs = refs[-ring:]
    for step in range(ring):
        outs[step][...] = kept[step] + other[step]


def pair_sum(kept, other, *after):
    ring = kept.shape[0]
    return pl.pallas_call(
        functools.partial(pair_kernel, ring),
        out_shape=[jax.ShapeDtypeStruct(kept.shape[1:], kept.dtype)] * ring,
        in_specs=[VMEM, VMEM] + [ANY] * len(after),
        out_specs=[VMEM] * ring,
        compiler_params=params(),
        cost_estimate=CHEAP,
        name="pair_sum",
    )(kept, other, *after)


def total_of(parts, columns):
    total = parts[0][:, columns].astype(jnp.float32)
    for part in parts[1:]:
        total = total + part[:, columns].astype(jnp.float32)
    return total.astype(jnp.bfloat16)


def total_kernel(block, *refs):
    out = refs[-1]
    for c in range(out.shape[1] // block):
        columns = slice(c * block, (c + 1) * block)
        out[:, columns] = total_of(refs[:-1], columns)


def add_up(parts, block):
    return pl.pallas_call(
        functools.partial(total_kernel, block),
        out_shape=jax.ShapeDtypeStruct(parts[0].shape, jnp.bfloat16),
        in_specs=[VMEM] * len(parts),
        out_specs=VMEM,
        compiler_params=params(),
        cost_estimate=CHEAP,
        name="add_up",
    )(*parts)


def take_kernel(start, part, *refs):
    out = refs[-1]
    out[...] = part[:, start : start + out.shape[1]]


def take(part, start, stop, *after):
    return pl.pallas_call(
        functools.partial(take_kernel, start),
        out_shape=jax.ShapeDtypeStruct((part.shape[0], stop - start), part.dtype),
        in_specs=[VMEM] + [ANY] * len(after),
        out_specs=VMEM,
        compiler_params=params(),
        cost_estimate=CHEAP,
        name="take",
    )(part, *after)


def plus_kernel(part, running, out):
    out[...] = part[:, : running.shape[1]] + running[...]


def plus(part, running):
    return pl.pallas_call(
        plus_kernel,
        out_shape=jax.ShapeDtypeStruct(running.shape, running.dtype),
        in_specs=[VMEM] * 2,
        out_specs=VMEM,
        compiler_params=params(),
        cost_estimate=CHEAP,
        name="plus",
    )(part, running)


def join_kernel(*refs):
    start = 0
    for ref in refs[:-1]:
        refs[-1][:, start : start + ref.shape[1]] = ref[...]
        start += ref.shape[1]


def join(pieces):
    width = sum(piece.shape[1] for piece in pieces)
    return pl.pallas_call(
        join_kernel,
        out_shape=jax.ShapeDtypeStruct((pieces[0].shape[0], width), pieces[0].dtype),
        in_specs=[VMEM] * len(pieces),
        out_specs=VMEM,
        compiler_params=params(),
        cost_estimate=CHEAP,
        name="join",
    )(*pieces)


def slots_kernel(pieces, block, n_parts, owners, *refs):
    parts, out = refs[:n_parts], refs[-1]
    out[...] = jnp.zeros_like(out)
    for c in range(pieces):
        out[owners[c]] = total_of(parts, slice(c * block, (c + 1) * block))


def fill_slots(parts, owners, n_fsdp, block, *after):
    strip, width = parts[0].shape
    return pl.pallas_call(
        functools.partial(slots_kernel, width // block, block, len(parts)),
        out_shape=jax.ShapeDtypeStruct((n_fsdp, strip, block), jnp.bfloat16),
        in_specs=[SMEM] + [VMEM] * len(parts) + [ANY] * len(after),
        out_specs=VMEM,
        compiler_params=params(),
        cost_estimate=CHEAP,
        name="fill_slots",
    )(owners, *parts, *after)


def precondition_kernel(g_ref, l_ref, r_ref, out_ref):
    slots, block, _ = l_ref.shape
    rows = g_ref.shape[0] // slots
    for b in range(slots):
        g = g_ref[b * rows : (b + 1) * rows].reshape(block, block)
        half = jnp.dot(l_ref[b], g, preferred_element_type=jnp.float32).astype(jnp.bfloat16)
        pre = jnp.dot(half, r_ref[b], preferred_element_type=jnp.float32)
        gfull = g.astype(jnp.float32)
        scale = jnp.sqrt(jnp.mean(gfull * gfull)) / jnp.sqrt(jnp.mean(pre * pre) + EPS)
        out_ref[b * rows : (b + 1) * rows] = (
            (scale * pre).astype(jnp.bfloat16).reshape(rows, *g_ref.shape[1:])
        )


def precondition(incoming, lroots, rroots):
    slots, block, _ = lroots.shape
    return pl.pallas_call(
        precondition_kernel,
        out_shape=jax.ShapeDtypeStruct(incoming.shape, jnp.bfloat16),
        in_specs=[VMEM] * 3,
        out_specs=VMEM,
        compiler_params=params(),
        cost_estimate=pl.CostEstimate(
            flops=4 * slots * block**3, bytes_accessed=8 * slots * block**2, transcendentals=0
        ),
        name="precondition",
    )(incoming, lroots, rroots)


def collect_kernel(pieces, block, owners, returned, update, sems):
    copies = [
        pltpu.make_async_copy(
            returned.at[owners[c]], update.at[:, pl.ds(c * block, block)], sems.at[c]
        )
        for c in range(pieces)
    ]
    for copy in copies:
        copy.start()
    for copy in copies:
        copy.wait()


def collect(returned, owners, pieces):
    n, strip, block = returned.shape
    return pl.pallas_call(
        functools.partial(collect_kernel, pieces, block),
        out_shape=jax.ShapeDtypeStruct((strip, pieces * block), returned.dtype),
        in_specs=[SMEM, ANY],
        out_specs=ANY,
        scratch_shapes=[pltpu.SemaphoreType.DMA((pieces,))],
        compiler_params=params(),
        name="collect",
    )(owners, returned)


def statistics(g, left, right):
    block = g.shape[0]
    gram_left = (
        lax.dot_general(g, g, (((1,), (1,)), ((), ())), preferred_element_type=jnp.float32) / block
    )
    gram_right = (
        lax.dot_general(g, g, (((0,), (0,)), ((), ())), preferred_element_type=jnp.float32) / block
    )
    return BETA * left + gram_left, BETA * right + gram_right


def on_device(grads, owner, left_stats, right_stats, left_root, right_root):
    strip = grads.shape[1]
    n_fsdp = lax.axis_size("fsdp")
    n_rep = lax.axis_size("rep")
    block = left_stats.shape[-1]
    slots = left_stats.shape[2]
    width = grads.shape[2] // n_rep
    pieces = width // block
    ring = n_rep // 2
    rep_index = lax.axis_index("rep")
    fsdp_index = lax.axis_index("fsdp")
    owners = lax.dynamic_slice(
        owner, (fsdp_index * strip // block, rep_index * pieces), (1, pieces)
    )[0]

    swap = [(i, i + 1 - 2 * (i % 2)) for i in range(n_rep)]
    other = lax.ppermute(groups(grads[0], ring, width, True), "rep", swap)
    parts = pair_sum(groups(grads[0], ring, width, False), other)

    def send_y(array, step):
        return lax.ppermute(array, "rep", [(i, (i + 2 * step) % n_rep) for i in range(n_rep)])

    def directly(parts):
        return add_up([parts[0]] + [send_y(parts[step], step) for step in Y_ORDER], block)

    def round_ring(parts):
        running = take(parts[0], 0, block)
        for part in parts[:0:-1]:
            running = plus(part, send_y(running, 1))
        running = send_y(running, 1)
        rest = [take(part, block, width, running) for part in parts]
        rest = add_up([rest[0]] + [send_y(rest[step], step) for step in Y_ORDER], block)
        return join([running, rest])

    total = lax.cond(rep_index % 2 == 0, directly, round_ring, parts)
    outgoing = fill_slots([total], owners, n_fsdp, block)
    incoming = lax.all_to_all(outgoing, "fsdp", split_axis=0, concat_axis=0, tiled=True)
    results = precondition(incoming, left_root[0, 0], right_root[0, 0])
    returned = lax.all_to_all(results, "fsdp", split_axis=0, concat_axis=0, tiled=True)
    new_l, new_r = jax.vmap(statistics)(
        incoming.reshape(slots, block, block), left_stats[0, 0], right_stats[0, 0]
    )
    update = collect(returned, owners, pieces)
    return (update, new_l[None, None], new_r[None, None])


def solution(mesh):
    in_specs = (
        P("rep", "fsdp", None),
        P(),
        P("rep", "fsdp", None, None, None),
        P("rep", "fsdp", None, None, None),
        P("rep", "fsdp", None, None, None),
        P("rep", "fsdp", None, None, None),
    )
    out_specs = (
        P("fsdp", "rep"),
        P("rep", "fsdp", None, None, None),
        P("rep", "fsdp", None, None, None),
    )
    return jax.shard_map(
        on_device, mesh=mesh, in_specs=in_specs, out_specs=out_specs, check_vma=False
    )
```

```python
import functools

import jax
import jax.numpy as jnp
from jax import lax
from jax.experimental import pallas as pl
from jax.experimental.pallas import tpu as pltpu
from jax.sharding import PartitionSpec as P

BETA = 0.9
EPS = 1e-06
Y_ORDER = (2, 1, 3)
PRE_PARTS = 2
CUTS = (0, 512)
VMEM_LIMIT = 24 * 1024 * 1024
ANY = pl.BlockSpec(memory_space=pl.ANY)
HBM = pl.BlockSpec(memory_space=pltpu.HBM)
VMEM = pl.BlockSpec(memory_space=pltpu.VMEM)
CHEAP = pl.CostEstimate(flops=1, bytes_accessed=1, transcendentals=0)
COPY = pl.CostEstimate(flops=1, bytes_accessed=2**21, transcendentals=0)
SMEM = pl.BlockSpec(memory_space=pltpu.SMEM)


def params(**kw):
    return pltpu.CompilerParams(vmem_limit_bytes=VMEM_LIMIT, **kw)


def groups_kernel(ring, width, other, shard, *refs):
    out, sems = refs[-2:]
    rep_index = lax.axis_index("rep")
    core = lax.rem(rep_index, 2)
    if other:
        core = 1 - core
    copies = []
    for step in range(ring):
        target = lax.rem(rep_index // 2 + step, ring)
        start = pl.multiple_of((2 * target + core) * width, width)
        copies.append(
            pltpu.make_async_copy(shard.at[:, pl.ds(start, width)], out.at[step], sems.at[step])
        )
    for copy in copies:
        copy.start()
    for copy in copies:
        copy.wait()


def groups(shard, ring, width, other, *after):
    return pl.pallas_call(
        functools.partial(groups_kernel, ring, width, other),
        out_shape=jax.ShapeDtypeStruct((ring, shard.shape[0], width), shard.dtype),
        in_specs=[HBM] + [ANY] * len(after),
        out_specs=VMEM,
        scratch_shapes=[pltpu.SemaphoreType.DMA((ring,))],
        compiler_params=params(),
        cost_estimate=COPY,
        name="groups",
    )(pltpu.with_memory_space_constraint(shard, pltpu.HBM), *after)


def pair_kernel(ring, kept, other, *refs):
    outs = refs[-ring:]
    for step in range(ring):
        outs[step][...] = kept[step] + other[step]


def pair_sum(kept, other, *after):
    ring = kept.shape[0]
    return pl.pallas_call(
        functools.partial(pair_kernel, ring),
        out_shape=[jax.ShapeDtypeStruct(kept.shape[1:], kept.dtype)] * ring,
        in_specs=[VMEM, VMEM] + [ANY] * len(after),
        out_specs=[VMEM] * ring,
        compiler_params=params(),
        cost_estimate=CHEAP,
        name="pair_sum",
    )(kept, other, *after)


def total_of(parts, columns):
    total = parts[0][:, columns].astype(jnp.float32)
    for part in parts[1:]:
        total = total + part[:, columns].astype(jnp.float32)
    return total.astype(jnp.bfloat16)


def total_kernel(block, *refs):
    out = refs[-1]
    for c in range(out.shape[1] // block):
        columns = slice(c * block, (c + 1) * block)
        out[:, columns] = total_of(refs[:-1], columns)


def add_up(parts, block):
    return pl.pallas_call(
        functools.partial(total_kernel, block),
        out_shape=jax.ShapeDtypeStruct(parts[0].shape, jnp.bfloat16),
        in_specs=[VMEM] * len(parts),
        out_specs=VMEM,
        compiler_params=params(),
        cost_estimate=CHEAP,
        name="add_up",
    )(*parts)


def take_kernel(start, part, *refs):
    out = refs[-1]
    out[...] = part[:, start : start + out.shape[1]]


def take(part, start, stop, *after):
    return pl.pallas_call(
        functools.partial(take_kernel, start),
        out_shape=jax.ShapeDtypeStruct((part.shape[0], stop - start), part.dtype),
        in_specs=[VMEM] + [ANY] * len(after),
        out_specs=VMEM,
        compiler_params=params(),
        cost_estimate=CHEAP,
        name="take",
    )(part, *after)


def plus_kernel(part, running, out):
    out[...] = part[:, : running.shape[1]] + running[...]


def plus(part, running):
    return pl.pallas_call(
        plus_kernel,
        out_shape=jax.ShapeDtypeStruct(running.shape, running.dtype),
        in_specs=[VMEM] * 2,
        out_specs=VMEM,
        compiler_params=params(),
        cost_estimate=CHEAP,
        name="plus",
    )(part, running)


def join_kernel(*refs):
    start = 0
    for ref in refs[:-1]:
        refs[-1][:, start : start + ref.shape[1]] = ref[...]
        start += ref.shape[1]


def join(pieces):
    width = sum(piece.shape[1] for piece in pieces)
    return pl.pallas_call(
        join_kernel,
        out_shape=jax.ShapeDtypeStruct((pieces[0].shape[0], width), pieces[0].dtype),
        in_specs=[VMEM] * len(pieces),
        out_specs=VMEM,
        compiler_params=params(),
        cost_estimate=CHEAP,
        name="join",
    )(*pieces)


def slots_kernel(pieces, block, n_parts, owners, *refs):
    parts, out = refs[:n_parts], refs[-1]
    out[...] = jnp.zeros_like(out)
    for c in range(pieces):
        out[owners[c]] = total_of(parts, slice(c * block, (c + 1) * block))


def fill_slots(parts, owners, n_fsdp, block, *after):
    strip, width = parts[0].shape
    return pl.pallas_call(
        functools.partial(slots_kernel, width // block, block, len(parts)),
        out_shape=jax.ShapeDtypeStruct((n_fsdp, strip, block), jnp.bfloat16),
        in_specs=[SMEM] + [VMEM] * len(parts) + [ANY] * len(after),
        out_specs=VMEM,
        compiler_params=params(),
        cost_estimate=CHEAP,
        name="fill_slots",
    )(owners, *parts, *after)


def precondition_kernel(g_ref, l_ref, r_ref, out_ref, held, sems):
    slots, block, _ = l_ref.shape
    rows = g_ref.shape[0] // slots
    part = rows // PRE_PARTS
    lines = block // PRE_PARTS
    copies = []
    for b in range(slots):
        g = g_ref[b * rows : (b + 1) * rows].reshape(block, block)
        half = jnp.dot(l_ref[b], g, preferred_element_type=jnp.float32).astype(jnp.bfloat16)
        pre = jnp.dot(half, r_ref[b], preferred_element_type=jnp.float32)
        gfull = g.astype(jnp.float32)
        scale = jnp.sqrt(jnp.mean(gfull * gfull)) / jnp.sqrt(jnp.mean(pre * pre) + EPS)
        for i in range(PRE_PARTS):
            scaled = scale * pre[i * lines : (i + 1) * lines]
            place = slice(b * rows + i * part, b * rows + (i + 1) * part)
            held[place] = scaled.astype(jnp.bfloat16).reshape(part, *g_ref.shape[1:])
            copies.append(
                pltpu.make_async_copy(held.at[place], out_ref.at[place], sems.at[len(copies)])
            )
            copies[-1].start()
    for copy in copies:
        copy.wait()


def precondition(incoming, lroots, rroots):
    slots, block, _ = lroots.shape
    return pl.pallas_call(
        precondition_kernel,
        out_shape=jax.ShapeDtypeStruct(incoming.shape, jnp.bfloat16),
        in_specs=[VMEM] * 3,
        out_specs=ANY,
        scratch_shapes=[
            pltpu.VMEM(incoming.shape, jnp.bfloat16),
            pltpu.SemaphoreType.DMA((slots * PRE_PARTS,)),
        ],
        compiler_params=params(),
        cost_estimate=pl.CostEstimate(
            flops=4 * slots * block**3, bytes_accessed=8 * slots * block**2, transcendentals=0
        ),
        name="precondition",
    )(incoming, lroots, rroots)


def collect_kernel(pieces, block, owners, returned, update, sems):
    copies = [
        pltpu.make_async_copy(
            returned.at[owners[c]], update.at[:, pl.ds(c * block, block)], sems.at[c]
        )
        for c in range(pieces)
    ]
    for copy in copies:
        copy.start()
    for copy in copies:
        copy.wait()


def collect(returned, owners, pieces):
    n, strip, block = returned.shape
    return pl.pallas_call(
        functools.partial(collect_kernel, pieces, block),
        out_shape=jax.ShapeDtypeStruct((strip, pieces * block), returned.dtype),
        in_specs=[SMEM, ANY],
        out_specs=ANY,
        scratch_shapes=[pltpu.SemaphoreType.DMA((pieces,))],
        compiler_params=params(),
        name="collect",
    )(owners, returned)


def statistics(g, left, right):
    block = g.shape[0]
    gram_left = (
        lax.dot_general(g, g, (((1,), (1,)), ((), ())), preferred_element_type=jnp.float32) / block
    )
    gram_right = (
        lax.dot_general(g, g, (((0,), (0,)), ((), ())), preferred_element_type=jnp.float32) / block
    )
    return BETA * left + gram_left, BETA * right + gram_right


def on_device(grads, owner, left_stats, right_stats, left_root, right_root):
    strip = grads.shape[1]
    n_fsdp = lax.axis_size("fsdp")
    n_rep = lax.axis_size("rep")
    block = left_stats.shape[-1]
    slots = left_stats.shape[2]
    width = grads.shape[2] // n_rep
    pieces = width // block
    ring = n_rep // 2
    rep_index = lax.axis_index("rep")
    fsdp_index = lax.axis_index("fsdp")
    owners = lax.dynamic_slice(
        owner, (fsdp_index * strip // block, rep_index * pieces), (1, pieces)
    )[0]

    swap = [(i, i + 1 - 2 * (i % 2)) for i in range(n_rep)]
    other = lax.ppermute(groups(grads[0], ring, width, True), "rep", swap)
    parts = pair_sum(groups(grads[0], ring, width, False), other)

    def send_y(array, step):
        return lax.ppermute(array, "rep", [(i, (i + 2 * step) % n_rep) for i in range(n_rep)])

    def directly(parts):
        return add_up([parts[0]] + [send_y(parts[step], step) for step in Y_ORDER], block)

    def in_turns(parts):
        done = []
        for start, stop in zip(CUTS, [*CUTS[1:], width], strict=True):
            some = [take(part, start, stop, *done[-1:]) for part in parts]
            done.append(add_up([some[0]] + [send_y(some[step], step) for step in Y_ORDER], block))
        return join(done)

    total = lax.cond(rep_index % 2 == 1, directly, in_turns, parts)
    outgoing = fill_slots([total], owners, n_fsdp, block)
    incoming = lax.all_to_all(outgoing, "fsdp", split_axis=0, concat_axis=0, tiled=True)
    results = precondition(incoming, left_root[0, 0], right_root[0, 0])
    returned = lax.all_to_all(results, "fsdp", split_axis=0, concat_axis=0, tiled=True)
    new_l, new_r = jax.vmap(statistics)(
        incoming.reshape(slots, block, block), left_stats[0, 0], right_stats[0, 0]
    )
    update = collect(returned, owners, pieces)
    return (update, new_l[None, None], new_r[None, None])


def solution(mesh):
    in_specs = (
        P("rep", "fsdp", None),
        P(),
        P("rep", "fsdp", None, None, None),
        P("rep", "fsdp", None, None, None),
        P("rep", "fsdp", None, None, None),
        P("rep", "fsdp", None, None, None),
    )
    out_specs = (
        P("fsdp", "rep"),
        P("rep", "fsdp", None, None, None),
        P("rep", "fsdp", None, None, None),
    )
    return jax.shard_map(
        on_device, mesh=mesh, in_specs=in_specs, out_specs=out_specs, check_vma=False
    )
```

```python
import functools

import jax
import jax.numpy as jnp
from jax import lax
from jax.experimental import pallas as pl
from jax.experimental.pallas import tpu as pltpu
from jax.sharding import PartitionSpec as P

BETA = 0.9
EPS = 1e-06
Y_ORDER = (2, 1, 3)
PRE_PARTS = 2
CUTS = (0, 512)
TURNS = ((2, 1), (3,))
VMEM_LIMIT = 24 * 1024 * 1024
ANY = pl.BlockSpec(memory_space=pl.ANY)
HBM = pl.BlockSpec(memory_space=pltpu.HBM)
VMEM = pl.BlockSpec(memory_space=pltpu.VMEM)
CHEAP = pl.CostEstimate(flops=1, bytes_accessed=1, transcendentals=0)
COPY = pl.CostEstimate(flops=1, bytes_accessed=2**21, transcendentals=0)
SMEM = pl.BlockSpec(memory_space=pltpu.SMEM)


def params(**kw):
    return pltpu.CompilerParams(vmem_limit_bytes=VMEM_LIMIT, **kw)


def groups_kernel(ring, width, other, shard, *refs):
    out, sems = refs[-2:]
    rep_index = lax.axis_index("rep")
    core = lax.rem(rep_index, 2)
    if other:
        core = 1 - core
    copies = []
    for step in range(ring):
        target = lax.rem(rep_index // 2 + step, ring)
        start = pl.multiple_of((2 * target + core) * width, width)
        copies.append(
            pltpu.make_async_copy(shard.at[:, pl.ds(start, width)], out.at[step], sems.at[step])
        )
    for copy in copies:
        copy.start()
    for copy in copies:
        copy.wait()


def groups(shard, ring, width, other, *after):
    return pl.pallas_call(
        functools.partial(groups_kernel, ring, width, other),
        out_shape=jax.ShapeDtypeStruct((ring, shard.shape[0], width), shard.dtype),
        in_specs=[HBM] + [ANY] * len(after),
        out_specs=VMEM,
        scratch_shapes=[pltpu.SemaphoreType.DMA((ring,))],
        compiler_params=params(),
        cost_estimate=COPY,
        name="groups",
    )(pltpu.with_memory_space_constraint(shard, pltpu.HBM), *after)


def pair_kernel(ring, kept, other, *refs):
    outs = refs[-ring:]
    for step in range(ring):
        outs[step][...] = kept[step] + other[step]


def pair_sum(kept, other, *after):
    ring = kept.shape[0]
    return pl.pallas_call(
        functools.partial(pair_kernel, ring),
        out_shape=[jax.ShapeDtypeStruct(kept.shape[1:], kept.dtype)] * ring,
        in_specs=[VMEM, VMEM] + [ANY] * len(after),
        out_specs=[VMEM] * ring,
        compiler_params=params(),
        cost_estimate=CHEAP,
        name="pair_sum",
    )(kept, other, *after)


def total_of(parts, columns):
    total = parts[0][:, columns].astype(jnp.float32)
    for part in parts[1:]:
        total = total + part[:, columns].astype(jnp.float32)
    return total.astype(jnp.bfloat16)


def total_kernel(block, *refs):
    out = refs[-1]
    for c in range(out.shape[1] // block):
        columns = slice(c * block, (c + 1) * block)
        out[:, columns] = total_of(refs[:-1], columns)


def add_up(parts, block):
    return pl.pallas_call(
        functools.partial(total_kernel, block),
        out_shape=jax.ShapeDtypeStruct(parts[0].shape, jnp.bfloat16),
        in_specs=[VMEM] * len(parts),
        out_specs=VMEM,
        compiler_params=params(),
        cost_estimate=CHEAP,
        name="add_up",
    )(*parts)


def take_kernel(start, part, *refs):
    out = refs[-1]
    out[...] = part[:, start : start + out.shape[1]]


def take(part, start, stop, *after):
    return pl.pallas_call(
        functools.partial(take_kernel, start),
        out_shape=jax.ShapeDtypeStruct((part.shape[0], stop - start), part.dtype),
        in_specs=[VMEM] + [ANY] * len(after),
        out_specs=VMEM,
        compiler_params=params(),
        cost_estimate=CHEAP,
        name="take",
    )(part, *after)


def plus_kernel(part, running, out):
    out[...] = part[:, : running.shape[1]] + running[...]


def plus(part, running):
    return pl.pallas_call(
        plus_kernel,
        out_shape=jax.ShapeDtypeStruct(running.shape, running.dtype),
        in_specs=[VMEM] * 2,
        out_specs=VMEM,
        compiler_params=params(),
        cost_estimate=CHEAP,
        name="plus",
    )(part, running)


def join_kernel(*refs):
    start = 0
    for ref in refs[:-1]:
        refs[-1][:, start : start + ref.shape[1]] = ref[...]
        start += ref.shape[1]


def join(pieces):
    width = sum(piece.shape[1] for piece in pieces)
    return pl.pallas_call(
        join_kernel,
        out_shape=jax.ShapeDtypeStruct((pieces[0].shape[0], width), pieces[0].dtype),
        in_specs=[VMEM] * len(pieces),
        out_specs=VMEM,
        compiler_params=params(),
        cost_estimate=CHEAP,
        name="join",
    )(*pieces)


def slots_kernel(pieces, block, n_parts, owners, *refs):
    parts, out = refs[:n_parts], refs[-1]
    out[...] = jnp.zeros_like(out)
    for c in range(pieces):
        out[owners[c]] = total_of(parts, slice(c * block, (c + 1) * block))


def fill_slots(parts, owners, n_fsdp, block, *after):
    strip, width = parts[0].shape
    return pl.pallas_call(
        functools.partial(slots_kernel, width // block, block, len(parts)),
        out_shape=jax.ShapeDtypeStruct((n_fsdp, strip, block), jnp.bfloat16),
        in_specs=[SMEM] + [VMEM] * len(parts) + [ANY] * len(after),
        out_specs=VMEM,
        compiler_params=params(),
        cost_estimate=CHEAP,
        name="fill_slots",
    )(owners, *parts, *after)


def precondition_kernel(g_ref, l_ref, r_ref, out_ref, held, sems):
    slots, block, _ = l_ref.shape
    rows = g_ref.shape[0] // slots
    part = rows // PRE_PARTS
    lines = block // PRE_PARTS
    copies = []
    for b in range(slots):
        g = g_ref[b * rows : (b + 1) * rows].reshape(block, block)
        half = jnp.dot(l_ref[b], g, preferred_element_type=jnp.float32).astype(jnp.bfloat16)
        pre = jnp.dot(half, r_ref[b], preferred_element_type=jnp.float32)
        gfull = g.astype(jnp.float32)
        scale = jnp.sqrt(jnp.mean(gfull * gfull)) / jnp.sqrt(jnp.mean(pre * pre) + EPS)
        for i in range(PRE_PARTS):
            scaled = scale * pre[i * lines : (i + 1) * lines]
            place = slice(b * rows + i * part, b * rows + (i + 1) * part)
            held[place] = scaled.astype(jnp.bfloat16).reshape(part, *g_ref.shape[1:])
            copies.append(
                pltpu.make_async_copy(held.at[place], out_ref.at[place], sems.at[len(copies)])
            )
            copies[-1].start()
    for copy in copies:
        copy.wait()


def precondition(incoming, lroots, rroots):
    slots, block, _ = lroots.shape
    return pl.pallas_call(
        precondition_kernel,
        out_shape=jax.ShapeDtypeStruct(incoming.shape, jnp.bfloat16),
        in_specs=[VMEM] * 3,
        out_specs=ANY,
        scratch_shapes=[
            pltpu.VMEM(incoming.shape, jnp.bfloat16),
            pltpu.SemaphoreType.DMA((slots * PRE_PARTS,)),
        ],
        compiler_params=params(),
        cost_estimate=pl.CostEstimate(
            flops=4 * slots * block**3, bytes_accessed=8 * slots * block**2, transcendentals=0
        ),
        name="precondition",
    )(incoming, lroots, rroots)


def collect_kernel(pieces, block, owners, returned, update, sems):
    copies = [
        pltpu.make_async_copy(
            returned.at[owners[c]], update.at[:, pl.ds(c * block, block)], sems.at[c]
        )
        for c in range(pieces)
    ]
    for copy in copies:
        copy.start()
    for copy in copies:
        copy.wait()


def collect(returned, owners, pieces):
    n, strip, block = returned.shape
    return pl.pallas_call(
        functools.partial(collect_kernel, pieces, block),
        out_shape=jax.ShapeDtypeStruct((strip, pieces * block), returned.dtype),
        in_specs=[SMEM, ANY],
        out_specs=ANY,
        scratch_shapes=[pltpu.SemaphoreType.DMA((pieces,))],
        compiler_params=params(),
        name="collect",
    )(owners, returned)


def statistics(g, left, right):
    block = g.shape[0]
    gram_left = (
        lax.dot_general(g, g, (((1,), (1,)), ((), ())), preferred_element_type=jnp.float32) / block
    )
    gram_right = (
        lax.dot_general(g, g, (((0,), (0,)), ((), ())), preferred_element_type=jnp.float32) / block
    )
    return BETA * left + gram_left, BETA * right + gram_right


def on_device(grads, owner, left_stats, right_stats, left_root, right_root):
    strip = grads.shape[1]
    n_fsdp = lax.axis_size("fsdp")
    n_rep = lax.axis_size("rep")
    block = left_stats.shape[-1]
    slots = left_stats.shape[2]
    width = grads.shape[2] // n_rep
    pieces = width // block
    ring = n_rep // 2
    rep_index = lax.axis_index("rep")
    fsdp_index = lax.axis_index("fsdp")
    owners = lax.dynamic_slice(
        owner, (fsdp_index * strip // block, rep_index * pieces), (1, pieces)
    )[0]

    swap = [(i, i + 1 - 2 * (i % 2)) for i in range(n_rep)]
    other = lax.ppermute(groups(grads[0], ring, width, True), "rep", swap)
    parts = pair_sum(groups(grads[0], ring, width, False), other)

    def send_y(array, step):
        return lax.ppermute(array, "rep", [(i, (i + 2 * step) % n_rep) for i in range(n_rep)])

    def directly(parts):
        return add_up([parts[0]] + [send_y(parts[step], step) for step in Y_ORDER], block)

    def in_turns(parts):
        done, after = [], []
        for start, stop in zip(CUTS, [*CUTS[1:], width], strict=True):
            terms = [take(parts[0], start, stop)]
            for turn in TURNS if start == 0 else (Y_ORDER,):
                some = [take(parts[step], start, stop, *after) for step in turn]
                terms += [send_y(part, step) for part, step in zip(some, turn, strict=True)]
                after = terms[-1:]
            done.append(add_up(terms, block))
        return join(done)

    total = lax.cond(rep_index % 2 == 1, directly, in_turns, parts)
    outgoing = fill_slots([total], owners, n_fsdp, block)
    incoming = lax.all_to_all(outgoing, "fsdp", split_axis=0, concat_axis=0, tiled=True)
    results = precondition(incoming, left_root[0, 0], right_root[0, 0])
    returned = lax.all_to_all(results, "fsdp", split_axis=0, concat_axis=0, tiled=True)
    new_l, new_r = jax.vmap(statistics)(
        incoming.reshape(slots, block, block), left_stats[0, 0], right_stats[0, 0]
    )
    update = collect(returned, owners, pieces)
    return (update, new_l[None, None], new_r[None, None])


def solution(mesh):
    in_specs = (
        P("rep", "fsdp", None),
        P(),
        P("rep", "fsdp", None, None, None),
        P("rep", "fsdp", None, None, None),
        P("rep", "fsdp", None, None, None),
        P("rep", "fsdp", None, None, None),
    )
    out_specs = (
        P("fsdp", "rep"),
        P("rep", "fsdp", None, None, None),
        P("rep", "fsdp", None, None, None),
    )
    return jax.shard_map(
        on_device, mesh=mesh, in_specs=in_specs, out_specs=out_specs, check_vma=False
    )
```

```python
import functools

import jax
import jax.numpy as jnp
from jax import lax
from jax.experimental import pallas as pl
from jax.experimental.pallas import tpu as pltpu
from jax.sharding import PartitionSpec as P

BETA = 0.9
EPS = 1e-06
Y_ORDER = (2, 1, 3)
PRE_PARTS = 2
CUTS = (0, 256)
STEP = 256
TURNS = ((2, 1), (3,))
VMEM_LIMIT = 24 * 1024 * 1024
ANY = pl.BlockSpec(memory_space=pl.ANY)
HBM = pl.BlockSpec(memory_space=pltpu.HBM)
VMEM = pl.BlockSpec(memory_space=pltpu.VMEM)
CHEAP = pl.CostEstimate(flops=1, bytes_accessed=1, transcendentals=0)
COPY = pl.CostEstimate(flops=1, bytes_accessed=2**21, transcendentals=0)
SMEM = pl.BlockSpec(memory_space=pltpu.SMEM)


def params(**kw):
    return pltpu.CompilerParams(vmem_limit_bytes=VMEM_LIMIT, **kw)


def groups_kernel(ring, width, other, shard, *refs):
    out, sems = refs[-2:]
    rep_index = lax.axis_index("rep")
    core = lax.rem(rep_index, 2)
    if other:
        core = 1 - core
    copies = []
    for step in range(ring):
        target = lax.rem(rep_index // 2 + step, ring)
        start = pl.multiple_of((2 * target + core) * width, width)
        copies.append(
            pltpu.make_async_copy(shard.at[:, pl.ds(start, width)], out.at[step], sems.at[step])
        )
    for copy in copies:
        copy.start()
    for copy in copies:
        copy.wait()


def groups(shard, ring, width, other, *after):
    return pl.pallas_call(
        functools.partial(groups_kernel, ring, width, other),
        out_shape=jax.ShapeDtypeStruct((ring, shard.shape[0], width), shard.dtype),
        in_specs=[HBM] + [ANY] * len(after),
        out_specs=VMEM,
        scratch_shapes=[pltpu.SemaphoreType.DMA((ring,))],
        compiler_params=params(),
        cost_estimate=COPY,
        name="groups",
    )(pltpu.with_memory_space_constraint(shard, pltpu.HBM), *after)


def pair_kernel(ring, kept, other, *refs):
    outs = refs[-ring:]
    for step in range(ring):
        outs[step][...] = kept[step] + other[step]


def pair_sum(kept, other, *after):
    ring = kept.shape[0]
    return pl.pallas_call(
        functools.partial(pair_kernel, ring),
        out_shape=[jax.ShapeDtypeStruct(kept.shape[1:], kept.dtype)] * ring,
        in_specs=[VMEM, VMEM] + [ANY] * len(after),
        out_specs=[VMEM] * ring,
        compiler_params=params(),
        cost_estimate=CHEAP,
        name="pair_sum",
    )(kept, other, *after)


def total_of(parts, columns):
    total = parts[0][:, columns].astype(jnp.float32)
    for part in parts[1:]:
        total = total + part[:, columns].astype(jnp.float32)
    return total.astype(jnp.bfloat16)


def total_kernel(block, *refs):
    out = refs[-1]
    for c in range(out.shape[1] // block):
        columns = slice(c * block, (c + 1) * block)
        out[:, columns] = total_of(refs[:-1], columns)


def add_up(parts, block):
    return pl.pallas_call(
        functools.partial(total_kernel, block),
        out_shape=jax.ShapeDtypeStruct(parts[0].shape, jnp.bfloat16),
        in_specs=[VMEM] * len(parts),
        out_specs=VMEM,
        compiler_params=params(),
        cost_estimate=CHEAP,
        name="add_up",
    )(*parts)


def take_kernel(start, part, *refs):
    out = refs[-1]
    out[...] = part[:, start : start + out.shape[1]]


def take(part, start, stop, *after):
    return pl.pallas_call(
        functools.partial(take_kernel, start),
        out_shape=jax.ShapeDtypeStruct((part.shape[0], stop - start), part.dtype),
        in_specs=[VMEM] + [ANY] * len(after),
        out_specs=VMEM,
        compiler_params=params(),
        cost_estimate=CHEAP,
        name="take",
    )(part, *after)


def plus_kernel(part, running, out):
    out[...] = part[:, : running.shape[1]] + running[...]


def plus(part, running):
    return pl.pallas_call(
        plus_kernel,
        out_shape=jax.ShapeDtypeStruct(running.shape, running.dtype),
        in_specs=[VMEM] * 2,
        out_specs=VMEM,
        compiler_params=params(),
        cost_estimate=CHEAP,
        name="plus",
    )(part, running)


def join_kernel(*refs):
    start = 0
    for ref in refs[:-1]:
        refs[-1][:, start : start + ref.shape[1]] = ref[...]
        start += ref.shape[1]


def join(pieces):
    width = sum(piece.shape[1] for piece in pieces)
    return pl.pallas_call(
        join_kernel,
        out_shape=jax.ShapeDtypeStruct((pieces[0].shape[0], width), pieces[0].dtype),
        in_specs=[VMEM] * len(pieces),
        out_specs=VMEM,
        compiler_params=params(),
        cost_estimate=CHEAP,
        name="join",
    )(*pieces)


def slots_kernel(pieces, block, n_parts, owners, *refs):
    parts, out = refs[:n_parts], refs[-1]
    out[...] = jnp.zeros_like(out)
    for c in range(pieces):
        out[owners[c]] = total_of(parts, slice(c * block, (c + 1) * block))


def fill_slots(parts, owners, n_fsdp, block, *after):
    strip, width = parts[0].shape
    return pl.pallas_call(
        functools.partial(slots_kernel, width // block, block, len(parts)),
        out_shape=jax.ShapeDtypeStruct((n_fsdp, strip, block), jnp.bfloat16),
        in_specs=[SMEM] + [VMEM] * len(parts) + [ANY] * len(after),
        out_specs=VMEM,
        compiler_params=params(),
        cost_estimate=CHEAP,
        name="fill_slots",
    )(owners, *parts, *after)


def precondition_kernel(g_ref, l_ref, r_ref, out_ref, held, sems):
    slots, block, _ = l_ref.shape
    rows = g_ref.shape[0] // slots
    part = rows // PRE_PARTS
    lines = block // PRE_PARTS
    copies = []
    for b in range(slots):
        g = g_ref[b * rows : (b + 1) * rows].reshape(block, block)
        half = jnp.dot(l_ref[b], g, preferred_element_type=jnp.float32).astype(jnp.bfloat16)
        pre = jnp.dot(half, r_ref[b], preferred_element_type=jnp.float32)
        gfull = g.astype(jnp.float32)
        scale = jnp.sqrt(jnp.mean(gfull * gfull)) / jnp.sqrt(jnp.mean(pre * pre) + EPS)
        for i in range(PRE_PARTS):
            scaled = scale * pre[i * lines : (i + 1) * lines]
            place = slice(b * rows + i * part, b * rows + (i + 1) * part)
            held[place] = scaled.astype(jnp.bfloat16).reshape(part, *g_ref.shape[1:])
            copies.append(
                pltpu.make_async_copy(held.at[place], out_ref.at[place], sems.at[len(copies)])
            )
            copies[-1].start()
    for copy in copies:
        copy.wait()


def precondition(incoming, lroots, rroots):
    slots, block, _ = lroots.shape
    return pl.pallas_call(
        precondition_kernel,
        out_shape=jax.ShapeDtypeStruct(incoming.shape, jnp.bfloat16),
        in_specs=[VMEM] * 3,
        out_specs=ANY,
        scratch_shapes=[
            pltpu.VMEM(incoming.shape, jnp.bfloat16),
            pltpu.SemaphoreType.DMA((slots * PRE_PARTS,)),
        ],
        compiler_params=params(),
        cost_estimate=pl.CostEstimate(
            flops=4 * slots * block**3, bytes_accessed=8 * slots * block**2, transcendentals=0
        ),
        name="precondition",
    )(incoming, lroots, rroots)


def collect_kernel(pieces, block, owners, returned, update, sems):
    copies = [
        pltpu.make_async_copy(
            returned.at[owners[c]], update.at[:, pl.ds(c * block, block)], sems.at[c]
        )
        for c in range(pieces)
    ]
    for copy in copies:
        copy.start()
    for copy in copies:
        copy.wait()


def collect(returned, owners, pieces):
    n, strip, block = returned.shape
    return pl.pallas_call(
        functools.partial(collect_kernel, pieces, block),
        out_shape=jax.ShapeDtypeStruct((strip, pieces * block), returned.dtype),
        in_specs=[SMEM, ANY],
        out_specs=ANY,
        scratch_shapes=[pltpu.SemaphoreType.DMA((pieces,))],
        compiler_params=params(),
        name="collect",
    )(owners, returned)


def statistics(g, left, right):
    block = g.shape[0]
    gram_left = (
        lax.dot_general(g, g, (((1,), (1,)), ((), ())), preferred_element_type=jnp.float32) / block
    )
    gram_right = (
        lax.dot_general(g, g, (((0,), (0,)), ((), ())), preferred_element_type=jnp.float32) / block
    )
    return BETA * left + gram_left, BETA * right + gram_right


def on_device(grads, owner, left_stats, right_stats, left_root, right_root):
    strip = grads.shape[1]
    n_fsdp = lax.axis_size("fsdp")
    n_rep = lax.axis_size("rep")
    block = left_stats.shape[-1]
    slots = left_stats.shape[2]
    width = grads.shape[2] // n_rep
    pieces = width // block
    ring = n_rep // 2
    rep_index = lax.axis_index("rep")
    fsdp_index = lax.axis_index("fsdp")
    owners = lax.dynamic_slice(
        owner, (fsdp_index * strip // block, rep_index * pieces), (1, pieces)
    )[0]

    swap = [(i, i + 1 - 2 * (i % 2)) for i in range(n_rep)]
    other = lax.ppermute(groups(grads[0], ring, width, True), "rep", swap)
    parts = pair_sum(groups(grads[0], ring, width, False), other)

    def send_y(array, step):
        return lax.ppermute(array, "rep", [(i, (i + 2 * step) % n_rep) for i in range(n_rep)])

    def directly(parts):
        return add_up([parts[0]] + [send_y(parts[step], step) for step in Y_ORDER], STEP)

    def in_turns(parts):
        done, after = [], []
        for start, stop in zip(CUTS, [*CUTS[1:], width], strict=True):
            terms = [take(parts[0], start, stop)]
            for turn in TURNS if start == 0 else (Y_ORDER,):
                some = [take(parts[step], start, stop, *after) for step in turn]
                terms += [send_y(part, step) for part, step in zip(some, turn, strict=True)]
                after = terms[-1:]
            done.append(add_up(terms, STEP))
        return join(done)

    total = lax.cond(rep_index % 2 == 1, directly, in_turns, parts)
    outgoing = fill_slots([total], owners, n_fsdp, block)
    incoming = lax.all_to_all(outgoing, "fsdp", split_axis=0, concat_axis=0, tiled=True)
    results = precondition(incoming, left_root[0, 0], right_root[0, 0])
    returned = lax.all_to_all(results, "fsdp", split_axis=0, concat_axis=0, tiled=True)
    new_l, new_r = jax.vmap(statistics)(
        incoming.reshape(slots, block, block), left_stats[0, 0], right_stats[0, 0]
    )
    update = collect(returned, owners, pieces)
    return (update, new_l[None, None], new_r[None, None])


def solution(mesh):
    in_specs = (
        P("rep", "fsdp", None),
        P(),
        P("rep", "fsdp", None, None, None),
        P("rep", "fsdp", None, None, None),
        P("rep", "fsdp", None, None, None),
        P("rep", "fsdp", None, None, None),
    )
    out_specs = (
        P("fsdp", "rep"),
        P("rep", "fsdp", None, None, None),
        P("rep", "fsdp", None, None, None),
    )
    return jax.shard_map(
        on_device, mesh=mesh, in_specs=in_specs, out_specs=out_specs, check_vma=False
    )
```
